32 devices in a mesh: grp: 2 (over y), row: 8 (over z, x), head: 2 (over core).
Axes of the slice: x: 2, y: 2, z: 4, core: 2. Of those that a mesh axis runs over, the one named last changes fastest.
Arguments:
- latent: bfloat16 [16, 256, 512], P(('grp', 'row')), parts along dimension 0, may hold values from -6 to 6
- weights: bfloat16 [512, 8, 512], P(None, None, 'head'), may hold values from -0.25 to 0.25
- cotangent: bfloat16 [16, 256, 512], P(('grp', 'row')), parts along dimension 0, may hold values from -6 to 6
Outputs:
- latent_grad: bfloat16 [16, 256, 512], P(('grp', 'row')), parts along dimension 0
- weight_grad: float32 [1024, 8, 512], P(('grp', 'row'), None, 'head'), parts along dimension 0
The draws below stay inside these ranges and needn't reach their ends.
There are 2 independent parts, one for each index of `grp`. The reference program is written for one: setup_inputs(seed, part) draws one part's arguments, and reference() takes and returns one part's arrays. A program takes and returns all parts, laid end to end along the dimension named above; an argument that names none is the same for every part. Nothing has to cross between parts.
All inputs are finite; a program needn't handle non-finite values.
Results may differ from the reference program's by a relative error of at most 0.03.
Values may be sent and summed in bfloat16 or wider, within the bound.
A program may use at most 64 MiB of HBM per device.

```python
import math
import jax
import jax.numpy as jnp
from jax import lax

HEADS = 8
HEAD_DIM = 64
CHAN = 512
SLOTS = 8
COLS = 256
HEIGHT = 8


def strengthened(values, rng, source, target, blocks, factor):
    owner, partner = [(jnp.arange(values.shape[position]) // (values.shape[position] // blocks)).reshape([-1 if axis == position else 1 for axis in range(values.ndim)]) for position in (source, target)]
    chosen = jax.random.permutation(rng, blocks)[partner]
    strong = (owner == chosen) | (owner == (partner + blocks // 2) % blocks)
    return jnp.where(strong, factor * values, values)


def levels(rng, dims, shards, smallest, top_value):
    def one(position, shards_of):
        draws = jax.random.uniform(jax.random.fold_in(jax.random.fold_in(rng, 6), position), (shards_of,), jnp.float32, smallest / len(shards), top_value / len(shards))
        return jnp.repeat(jnp.exp(draws), dims[position] // shards_of).reshape((-1,) + (1,) * (len(dims) - position - 1))

    factor_of = one(*shards[0])
    for cut in shards[1:]:
        factor_of = factor_of * one(*cut)
    return factor_of


def gaussian(own_key, dims, spread, limit, split=(), held_as=jnp.bfloat16):
    entries = spread * jax.random.normal(own_key, dims, jnp.float32)
    if split:
        entries = entries * levels(own_key, dims, split, -0.22, 0.18)
    return jnp.clip(entries, -limit, limit).astype(held_as)


def bell_draw_with(key, dims, deviation, most, split, heavy, dtype=jnp.bfloat16):
    entries = deviation * jax.random.normal(key, dims, jnp.float32)
    if split:
        entries = entries * levels(key, dims, split, -0.22, 0.18)
    return jnp.clip(strengthened(entries, jax.random.fold_in(key, 3), *heavy), -most, most).astype(dtype)


def setup_inputs(seed: int = 0, part: int = 0) -> dict:
    seeds = jax.random.split(jax.random.key(seed), 4)
    own_keys = jax.random.split(jax.random.fold_in(seeds[3], part), 4)
    return {
        "latent": bell_draw_with(own_keys[0], (HEIGHT, COLS, CHAN), 1.0, 6.0, ((0, 8),), (0, 2, 8, 2.0)),
        "weights": gaussian(seeds[1], (CHAN, SLOTS, CHAN), CHAN ** -0.5, 0.25, ((2, 2),)),
        "cotangent": bell_draw_with(own_keys[2], (HEIGHT, COLS, CHAN), 1.0, 6.0, ((0, 8),), (0, 2, 8, 2.0)),
    }


epsilon = 1e-06

def normalize(values):
    shaped = values.reshape(values.shape[0], HEADS, HEAD_DIM)
    inverse = lax.rsqrt(lax.optimization_barrier(jnp.mean(shaped * shaped, axis=-1, keepdims=True)) + epsilon)
    return (shaped * inverse, inverse)

def sequence_core(query, key, value):
    logit_scale = 2.0 / math.sqrt(HEAD_DIM)
    query_n, query_r = normalize(query)
    key_n, key_r = normalize(key)
    query_batched = query_n.astype(jnp.bfloat16)
    key_batched = key_n.astype(jnp.bfloat16)
    value_batched = value.reshape(value.shape[0], HEADS, HEAD_DIM)
    attention_logits = logit_scale * jnp.einsum('wru,fru->rwf', query_batched.astype(jnp.float32), key_batched.astype(jnp.float32))
    expo = jnp.exp(attention_logits)
    probs = expo / lax.optimization_barrier(jnp.sum(expo, axis=-1, keepdims=True))
    probability_batched = probs.astype(jnp.bfloat16)
    attention_output = jnp.einsum('xkr,rxt->kxt', probability_batched.astype(jnp.float32), value_batched.astype(jnp.float32)).astype(jnp.bfloat16)
    return ((query_n, query_r, query_batched, key_n, key_r, key_batched, value_batched, probs, probability_batched), attention_output)

def forward_sequence(item):
    query, key, value = item
    saved, attention_output = sequence_core(query, key, value)
    return attention_output.reshape(query.shape[0], CHAN)

def backward_sequence(item):
    query, key, value, grad_att = item
    saved, attention_output = sequence_core(query, key, value)
    query_n, query_r, query_batched, key_n, key_r, key_batched, value_batched, probs, probability_batched = saved
    logit_scale = 2.0 / math.sqrt(HEAD_DIM)
    length = query.shape[0]
    gradient_attention_input = grad_att.reshape(length, HEADS, HEAD_DIM).astype(jnp.float32)
    gradient_value_rows = jnp.einsum('fir,ife->rfe', probability_batched.astype(jnp.float32), gradient_attention_input).astype(jnp.bfloat16)
    gradient_probability = jnp.einsum('wru,fru->rwf', gradient_attention_input, value_batched.astype(jnp.float32))
    delta = lax.optimization_barrier(jnp.sum(probs * gradient_probability, axis=-1, keepdims=True))
    gradient_logits = (probs * (gradient_probability - delta)).astype(jnp.bfloat16).astype(jnp.float32)
    gradient_normed_query = logit_scale * jnp.einsum('xkr,rxt->kxt', gradient_logits, key_batched.astype(jnp.float32))
    gradient_normed_key = logit_scale * jnp.einsum('fir,ife->rfe', gradient_logits, query_batched.astype(jnp.float32))
    grad_query = (query_r * (gradient_normed_query - query_n * lax.optimization_barrier(jnp.mean(gradient_normed_query * query_n, axis=-1, keepdims=True)))).astype(jnp.bfloat16)
    grad_key = (key_r * (gradient_normed_key - key_n * lax.optimization_barrier(jnp.mean(gradient_normed_key * key_n, axis=-1, keepdims=True)))).astype(jnp.bfloat16)
    return (attention_output.reshape(length, CHAN), grad_query.reshape(length, CHAN), grad_key.reshape(length, CHAN), gradient_value_rows.reshape(length, CHAN))

def projections(flat, weights, first):
    query = jnp.dot(flat, weights[:, first, :], preferred_element_type=jnp.float32)
    key = jnp.dot(flat, weights[:, first + 1, :], preferred_element_type=jnp.float32)
    value = jnp.dot(flat, weights[:, first + 2, :], preferred_element_type=jnp.float32).astype(jnp.bfloat16)
    return (query, key, value)

def layer_forward(inputs, weights, first):
    count, length, width = inputs.shape
    query, key, value = projections(inputs.reshape(count * length, width), weights, first)
    shape_three = (count, length, width)
    attention_output = lax.map(forward_sequence, (query.reshape(shape_three), key.reshape(shape_three), value.reshape(shape_three)))
    mixed = jnp.dot(attention_output.reshape(count * length, width), weights[:, first + 3, :].T, preferred_element_type=jnp.float32)
    return (inputs.astype(jnp.float32) + mixed.reshape(shape_three)).astype(jnp.bfloat16)

def layer_backward(inputs, upstream, weights, first):
    count, length, width = inputs.shape
    flat = inputs.reshape(count * length, width)
    grad_flat = upstream.reshape(count * length, width)
    query, key, value = projections(flat, weights, first)
    grad_att = jnp.dot(grad_flat, weights[:, first + 3, :], preferred_element_type=jnp.float32).astype(jnp.bfloat16)
    shape_three = (count, length, width)
    attention_output, grad_query, grad_key, gradient_value_rows = lax.map(backward_sequence, (query.reshape(shape_three), key.reshape(shape_three), value.reshape(shape_three), grad_att.reshape(shape_three)))
    attention_output = attention_output.reshape(count * length, width)
    grad_query = grad_query.reshape(count * length, width)
    grad_key = grad_key.reshape(count * length, width)
    gradient_value_rows = gradient_value_rows.reshape(count * length, width)
    back = jnp.dot(grad_query, weights[:, first, :].T, preferred_element_type=jnp.float32)
    back = back + jnp.dot(grad_key, weights[:, first + 1, :].T, preferred_element_type=jnp.float32)
    back = back + jnp.dot(gradient_value_rows, weights[:, first + 2, :].T, preferred_element_type=jnp.float32)
    grad_in = (upstream.astype(jnp.float32) + back.reshape(shape_three)).astype(jnp.bfloat16)
    grads = jnp.stack([jnp.dot(flat.T, grad_query, preferred_element_type=jnp.float32), jnp.dot(flat.T, grad_key, preferred_element_type=jnp.float32), jnp.dot(flat.T, gradient_value_rows, preferred_element_type=jnp.float32), jnp.dot(grad_flat.T, attention_output, preferred_element_type=jnp.float32)], axis=1)
    return (grad_in, grads)

def reference(latent, weights, cotangent):
    first_out = layer_forward(latent, weights, 0)
    column_in = jnp.transpose(first_out, (1, 0, 2))
    column_grad = jnp.transpose(cotangent, (1, 0, 2))
    grad_mid, grads_col = layer_backward(column_in, column_grad, weights, 4)
    grad_first = jnp.transpose(grad_mid, (1, 0, 2))
    latent_grad, grads_row = layer_backward(latent, grad_first, weights, 0)
    weight_grad = jnp.concatenate([grads_row, grads_col], axis=1) / math.sqrt(HEIGHT * COLS)
    return (latent_grad, weight_grad)
```

```python
import functools
import math

import jax
import jax.numpy as jnp
from jax import lax
from jax.experimental import pallas as pl
from jax.experimental.pallas import tpu as pltpu
from jax.sharding import PartitionSpec as P

HEAD_DIM = 64


epsilon = 1e-06


def index_pair(pattern):
    return (pattern + "hd", pattern.replace("l", "m") + "hd")


def head_norm(values):
    inverse = lax.rsqrt(jnp.mean(values * values, axis=-1, keepdims=True) + epsilon)
    return (values * inverse, inverse)


def three_maps(weights, first):
    width = weights.shape[0]
    return weights[:, first : first + 3, :].reshape(width, 3 * weights.shape[2])


def attend_local(inputs, weights, first, pattern):
    outer, inner, width = inputs.shape
    local = weights.shape[2]
    heads_here = local // HEAD_DIM
    logit_scale = 2.0 / math.sqrt(HEAD_DIM)
    flat = inputs.reshape(outer * inner, width)
    joined = jnp.dot(flat, three_maps(weights, first), preferred_element_type=jnp.float32)
    shaped = joined.reshape(outer, inner, 3, heads_here, HEAD_DIM)
    query_n, query_r = head_norm(shaped[:, :, 0])
    key_n, key_r = head_norm(shaped[:, :, 1])
    query_batched = query_n.astype(jnp.bfloat16)
    key_batched = key_n.astype(jnp.bfloat16)
    value_batched = shaped[:, :, 2].astype(jnp.bfloat16)
    query_ix, key_ix = index_pair(pattern)
    attention_logits = logit_scale * jnp.einsum(
        query_ix + "," + key_ix + "->shlm",
        query_batched,
        key_batched,
        preferred_element_type=jnp.float32,
    )
    expo = jnp.exp(attention_logits)
    probs = expo / jnp.sum(expo, axis=-1, keepdims=True)
    probability_batched = probs.astype(jnp.bfloat16)
    attention_output = jnp.einsum(
        "shlm," + key_ix + "->" + query_ix,
        probability_batched,
        value_batched,
        preferred_element_type=jnp.float32,
    ).astype(jnp.bfloat16)
    saved = (
        query_n,
        query_r,
        query_batched,
        key_n,
        key_r,
        key_batched,
        value_batched,
        probs,
        probability_batched,
    )
    return (flat, saved, attention_output.reshape(outer * inner, local))


def attend_back(saved, upstream, weights, first, pattern):
    outer, inner, width = upstream.shape
    local = weights.shape[2]
    heads_here = local // HEAD_DIM
    logit_scale = 2.0 / math.sqrt(HEAD_DIM)
    (
        query_n,
        query_r,
        query_batched,
        key_n,
        key_r,
        key_batched,
        value_batched,
        probs,
        probability_batched,
    ) = saved
    query_ix, key_ix = index_pair(pattern)
    grad_flat = upstream.reshape(outer * inner, width)
    grad_att = jnp.dot(
        grad_flat, weights[:, first + 3, :], preferred_element_type=jnp.float32
    ).astype(jnp.bfloat16)
    grad_att = grad_att.reshape(outer, inner, heads_here, HEAD_DIM)
    gradient_value_rows = jnp.einsum(
        "shlm," + query_ix + "->" + key_ix,
        probability_batched,
        grad_att,
        preferred_element_type=jnp.float32,
    ).astype(jnp.bfloat16)
    gradient_probability = jnp.einsum(
        query_ix + "," + key_ix + "->shlm",
        grad_att,
        value_batched,
        preferred_element_type=jnp.float32,
    )
    delta = jnp.sum(probs * gradient_probability, axis=-1, keepdims=True)
    gradient_logits = (probs * (gradient_probability - delta)).astype(jnp.bfloat16)
    gradient_normed_query = logit_scale * jnp.einsum(
        "shlm," + key_ix + "->" + query_ix,
        gradient_logits,
        key_batched,
        preferred_element_type=jnp.float32,
    )
    gradient_normed_key = logit_scale * jnp.einsum(
        "shlm," + query_ix + "->" + key_ix,
        gradient_logits,
        query_batched,
        preferred_element_type=jnp.float32,
    )
    grad_query = (
        query_r
        * (
            gradient_normed_query
            - query_n * jnp.mean(gradient_normed_query * query_n, axis=-1, keepdims=True)
        )
    ).astype(jnp.bfloat16)
    grad_key = (
        key_r
        * (
            gradient_normed_key
            - key_n * jnp.mean(gradient_normed_key * key_n, axis=-1, keepdims=True)
        )
    ).astype(jnp.bfloat16)
    stacked = jnp.stack([grad_query, grad_key, gradient_value_rows], axis=2).reshape(
        outer * inner, 3 * local
    )
    partial_in = lax.dot_general(
        stacked,
        three_maps(weights, first),
        (((1,), (1,)), ((), ())),
        preferred_element_type=jnp.float32,
    )
    return (partial_in, stacked, grad_flat)


def weight_terms(flat, stacked, grad_flat, attention_output, count):
    contract = (((0,), (0,)), ((), ()))
    three = lax.dot_general(flat, stacked, contract, preferred_element_type=jnp.float32)
    last = lax.dot_general(
        grad_flat, attention_output, contract, preferred_element_type=jnp.float32
    )
    return jnp.concatenate((three.reshape(count, 3, -1), last.reshape(count, 1, -1)), 1)


def head_sum(partial_value):
    return lax.psum(partial_value.astype(jnp.bfloat16), "head").astype(jnp.float32)


def on_device(latent, weights, cotangent):
    rows, cols, width = latent.shape
    rows_here = width // lax.axis_size("row")
    flat_row, saved_row, attended_row = attend_local(latent, weights, 0, "sl")
    mixed = head_sum(
        lax.dot_general(
            attended_row,
            weights[:, 3, :],
            (((1,), (1,)), ((), ())),
            preferred_element_type=jnp.float32,
        )
    )
    first_out = (latent.astype(jnp.float32) + mixed.reshape(rows, cols, width)).astype(jnp.bfloat16)
    columns, cotangent_cols = (
        lax.all_to_all(first_out, "row", split_axis=1, concat_axis=0, tiled=True),
        lax.all_to_all(cotangent, "row", split_axis=1, concat_axis=0, tiled=True),
    )
    height = columns.shape[0]
    flat_col, saved_col, attended_col = attend_local(columns, weights, 4, "ls")
    partial_col, stacked_col, grad_col = attend_back(saved_col, cotangent_cols, weights, 4, "ls")
    grad_mid = (
        cotangent_cols.astype(jnp.float32) + head_sum(partial_col).reshape(columns.shape)
    ).astype(jnp.bfloat16)
    grad_first = lax.all_to_all(grad_mid, "row", split_axis=0, concat_axis=1, tiled=True)
    partial_row, stacked_row, grad_row = attend_back(saved_row, grad_first, weights, 0, "sl")
    latent_grad = (
        grad_first.astype(jnp.float32) + head_sum(partial_row).reshape(latent.shape)
    ).astype(jnp.bfloat16)
    summed = lax.psum_scatter(
        jnp.concatenate(
            (
                weight_terms(
                    flat_row, stacked_row, grad_row, attended_row, rows_here * lax.axis_size("row")
                ),
                weight_terms(
                    flat_col, stacked_col, grad_col, attended_col, rows_here * lax.axis_size("row")
                ),
            ),
            1,
        ),
        "row",
        scatter_dimension=0,
        tiled=True,
    )
    weight_grad = summed * (1.0 / math.sqrt(height * cols))
    return (latent_grad, weight_grad)


MESH = pl.DeviceIdType.MESH
F32, BF16 = jnp.float32, jnp.bfloat16


def mm(left, right):
    return jnp.dot(left, right, preferred_element_type=F32)


def mm_t(left, right):
    return lax.dot_general(left, right, (((1,), (1,)), ((), ())), preferred_element_type=F32)


def t_mm(left, right):
    return lax.dot_general(left, right, (((0,), (0,)), ((), ())), preferred_element_type=F32)


def fused(
    n, scale, x_ref, w_ref, ct_ref, lat_ref, wg_ref,
    gcol, ycol, gmid, ysend, dsend, hsend, hrecv, fsend, frecv,
    norm_s, inv_s, qkv_s, probs_s, att_s, grads_s, dstack, pstack,
    xs, xr, zs, zr,
    a_send, a_recv, h_send, h_recv, x_send, x_recv, z_send, z_recv,
):
    me, core = lax.axis_index("row"), lax.axis_index("head")
    other = 1 - core
    count, width = x_ref.shape
    local = w_ref.shape[2]
    block, half = count // n, width // 2
    heads = local // HEAD_DIM
    logit_scale = 2.0 / math.sqrt(HEAD_DIM)
    pairs = n // 2
    my_x, my_z = lax.rem(me, 2), me // 2
    rows_here = width // n

    peers = [(me, other)]
    for step in range(1, n):
        for which in (core, other):
            peers.append((lax.rem(me + step, n), which))

    def rows_of(position):
        return pl.ds(pl.multiple_of(position * block, block), block)

    def half_of(which):
        return pl.ds(pl.multiple_of(which * half, half), half)

    def exchange_copy(phase, index, src, dst, source, target):
        row, which = source
        return pltpu.make_async_remote_copy(
            src_ref=src,
            dst_ref=dst.at[which, rows_of(row), :],
            send_sem=a_send.at[phase, index],
            recv_sem=a_recv.at[phase, which * n + row],
            device_id={"row": target[0], "head": target[1]},
            device_id_type=MESH,
        )

    def exchange_start(phase, view, dst):
        copies = []
        for index, target in enumerate(peers):
            copy = exchange_copy(phase, index, view(target[0]), dst, (me, core), target)
            copy.start()
            copies.append(copy)
        return copies

    def exchange_wait(phase, view, dst):
        for index, source in enumerate(peers):
            exchange_copy(phase, index, view(me), dst, source, source).wait_recv()

    def head_copy(phase, src, dst):
        return pltpu.make_async_remote_copy(
            src_ref=src, dst_ref=dst, send_sem=h_send.at[phase], recv_sem=h_recv.at[phase],
            device_id={"row": me, "head": other}, device_id_type=MESH,
        )

    def x_copy(layer, slot):
        return pltpu.make_async_remote_copy(
            src_ref=xs.at[layer, slot, 1 - my_x], dst_ref=xr.at[layer, slot],
            send_sem=x_send.at[layer, slot], recv_sem=x_recv.at[layer, slot],
            device_id={"row": me + 1 - 2 * my_x, "head": core}, device_id_type=MESH,
        )

    def z_copy(layer, slot, index, source_z, target_z):
        return pltpu.make_async_remote_copy(
            src_ref=zs.at[layer, slot, target_z], dst_ref=zr.at[layer, slot, source_z],
            send_sem=z_send.at[layer, slot, index], recv_sem=z_recv.at[layer, slot, source_z],
            device_id={"row": 2 * target_z + my_x, "head": core}, device_id_type=MESH,
        )

    def scatter_first(layer, slot, product):
        rounded = product.astype(BF16)
        for target in range(n):
            xs[layer, slot, target % 2, target // 2] = rounded[
                target * rows_here : (target + 1) * rows_here
            ]
        x_copy(layer, slot).start()

    def scatter_second(layer, slot):
        x_copy(layer, slot).wait_recv()
        total = xs[layer, slot, my_x].astype(F32) + xr[layer, slot].astype(F32)
        zs[layer, slot] = total.astype(BF16)
        for step in range(1, pairs):
            z_copy(layer, slot, step, my_z, lax.rem(my_z + step, pairs)).start()

    def scatter_last(layer, slot):
        total = zs[layer, slot, my_z].astype(F32)
        for step in range(1, pairs):
            source = lax.rem(my_z + step, pairs)
            z_copy(layer, slot, step, source, source).wait_recv()
            total = total + zr[layer, slot, source].astype(F32)
        wg_ref[:, 4 * layer + slot, :] = total * scale

    lane = lax.broadcasted_iota(jnp.int32, (1, local), 1) // HEAD_DIM
    head_mask = [jnp.where(lane == head, 1.0, 0.0).astype(BF16) for head in range(heads)]
    spread = jnp.where(
        lax.broadcasted_iota(jnp.int32, (local, local), 0) // HEAD_DIM
        == lax.broadcasted_iota(jnp.int32, (local, local), 1) // HEAD_DIM,
        1.0 / HEAD_DIM, 0.0,
    ).astype(BF16)
    spread_twice = jnp.concatenate([spread, spread], 0)

    def head_mean(values):
        high = values.astype(BF16)
        low = (values - high.astype(F32)).astype(BF16)
        return mm(jnp.concatenate([high, low], 1), spread_twice)

    def masked(values):
        return jnp.concatenate([values * mask for mask in head_mask], 0)

    def forward(layer, z):
        query, key, value = (mm(z, w_ref[4 * layer + i]) for i in range(3))
        both = jnp.concatenate([query, key], 0)
        inverse = lax.rsqrt(head_mean(both * both) + epsilon)
        normed = both * inverse
        norm_s[layer] = normed
        inv_s[layer] = inverse
        qkv_s[layer, 0] = normed[:count].astype(BF16)
        qkv_s[layer, 1] = normed[count:].astype(BF16)
        qkv_s[layer, 2] = value.astype(BF16)
        query_b, key_b = qkv_s[layer, 0], qkv_s[layer, 1]
        keep = None
        if layer == 1:
            keep = jnp.where(
                lax.rem(lax.broadcasted_iota(jnp.int32, (count, count), 0), block)
                == lax.rem(lax.broadcasted_iota(jnp.int32, (count, count), 1), block),
                1.0, 0.0,
            )
        for head in range(heads):
            expo = jnp.exp(logit_scale * mm_t(query_b * head_mask[head], key_b))
            if keep is not None:
                expo = expo * keep
            probs = expo * (1.0 / jnp.sum(expo, axis=-1, keepdims=True))
            probs_s[layer, head] = probs
            pstack[layer, head * count : (head + 1) * count, :] = probs.astype(BF16)
        wide = jnp.concatenate(
            [pstack[layer, head * count : (head + 1) * count, :] for head in range(heads)], 1
        )
        att_s[layer] = mm(wide, masked(qkv_s[layer, 2])).astype(BF16)

    def backward(layer, grad, after_value):
        query_b, key_b, value_b = qkv_s[layer, 0], qkv_s[layer, 1], qkv_s[layer, 2]
        grad_att = mm(grad, w_ref[4 * layer + 3]).astype(BF16)
        grads_s[layer, 2] = t_mm(pstack[layer], masked(grad_att)).astype(BF16)
        after_value()
        for head in range(heads):
            grad_probs = mm_t(grad_att * head_mask[head], value_b)
            probs = probs_s[layer, head]
            delta = jnp.sum(probs * grad_probs, axis=-1, keepdims=True)
            dstack[head * count : (head + 1) * count, :] = (
                probs * (grad_probs - delta)
            ).astype(BF16)
        wide = jnp.concatenate(
            [dstack[head * count : (head + 1) * count, :] for head in range(heads)], 1
        )
        grad_query = mm(wide, masked(key_b))
        grad_key = t_mm(dstack[...], masked(query_b))
        grads = logit_scale * jnp.concatenate([grad_query, grad_key], 0)
        normed = norm_s[layer]
        out = (inv_s[layer] * (grads - normed * head_mean(grads * normed))).astype(BF16)
        grads_s[layer, 0] = out[:count]
        grads_s[layer, 1] = out[count:]

    def input_grad(layer, which):
        total = mm_t(grads_s[layer, 0], w_ref[4 * layer, half_of(which), :])
        for i in (1, 2):
            total = total + mm_t(grads_s[layer, i], w_ref[4 * layer + i, half_of(which), :])
        return total

    def joined(ref):
        return jnp.concatenate([ref[0], ref[1]], 1)

    barrier = pltpu.get_barrier_semaphore()
    for row, which in peers:
        pl.semaphore_signal(
            barrier, inc=1, device_id={"row": row, "head": which}, device_id_type=MESH
        )
    pl.semaphore_wait(barrier, len(peers))

    def ct_view(row):
        return ct_ref.at[rows_of(row), half_of(core)]

    def y_view(row):
        return ysend.at[rows_of(row), :]

    def d_view(row):
        return dsend.at[rows_of(row), :]

    copies = exchange_start(0, ct_view, gcol)
    gcol[core, rows_of(me), :] = ct_ref[rows_of(me), half_of(core)]

    forward(0, x_ref[...])
    hsend[0] = mm_t(att_s[0], w_ref[3, half_of(other), :]).astype(BF16)
    first_half = head_copy(0, hsend.at[0], hrecv.at[0])
    first_half.start()
    mixed = mm_t(att_s[0], w_ref[3, half_of(core), :]) + x_ref[:, half_of(core)].astype(F32)
    first_half.wait_recv()
    ysend[...] = (mixed + hrecv[0].astype(F32)).astype(BF16)
    copies += exchange_start(1, y_view, ycol)
    ycol[core, rows_of(me), :] = ysend[rows_of(me), :]

    exchange_wait(0, ct_view, gcol)
    exchange_wait(1, y_view, ycol)
    columns = joined(ycol)
    forward(1, columns)
    backward(1, joined(gcol), lambda: None)
    hsend[1] = input_grad(1, other).astype(BF16)
    second_half = head_copy(1, hsend.at[1], hrecv.at[1])
    second_half.start()
    mixed = input_grad(1, core) + gcol[core].astype(F32)
    second_half.wait_recv()
    dsend[...] = (mixed + hrecv[1].astype(F32)).astype(BF16)
    copies += exchange_start(2, d_view, gmid)
    gmid[core, rows_of(me), :] = dsend[rows_of(me), :]
    turned = joined(ycol).T
    for slot in range(3):
        scatter_first(1, slot, mm(turned, grads_s[1, slot]))
    scatter_first(1, 3, mm(joined(gcol).T, att_s[1]))

    exchange_wait(2, d_view, gmid)
    grad_first = joined(gmid)
    scatter_first(0, 3, mm(grad_first.T, att_s[0]))

    def after_value():
        scatter_first(0, 2, mm(x_ref[...].T, grads_s[0, 2]))
        for slot in range(4):
            scatter_second(1, slot)

    backward(0, grad_first, after_value)
    turned = x_ref[...].T
    scatter_first(0, 0, mm(turned, grads_s[0, 0]))
    scatter_first(0, 1, mm(turned, grads_s[0, 1]))
    for which in range(2):
        fsend[which] = input_grad(0, which).astype(BF16)
    full = head_copy(2, fsend, frecv)
    full.start()
    scatter_second(0, 3)
    scatter_second(0, 2)
    full.wait_recv()
    for which in range(2):
        lat_ref[:, which * half : (which + 1) * half] = (
            gmid[which].astype(F32) + (fsend[which].astype(F32) + frecv[which].astype(F32))
        ).astype(BF16)
    for slot in range(4):
        scatter_last(1, slot)
    scatter_second(0, 0)
    scatter_second(0, 1)
    for slot in (3, 2, 0, 1):
        scatter_last(0, slot)

    for copy in copies:
        copy.wait_send()
    for copy in (first_half, second_half, full):
        copy.wait_send()
    for layer in range(2):
        for slot in range(4):
            x_copy(layer, slot).wait_send()
            for step in range(1, pairs):
                z_copy(layer, slot, step, my_z, lax.rem(my_z + step, pairs)).wait_send()


def fused_call(latent, weights, cotangent):
    n = lax.axis_size("row")
    _, count, width = latent.shape
    local = weights.shape[2]
    heads, block, half, rows_here = local // HEAD_DIM, count // n, width // 2, width // n
    scale = 1.0 / math.sqrt(n * count)
    vmem = pl.BlockSpec(memory_space=pltpu.VMEM)
    dma = pltpu.SemaphoreType.DMA
    halves = pltpu.VMEM((2, count, half), BF16)
    latent_grad, weight_grad = pl.pallas_call(
        functools.partial(fused, n, scale),
        out_shape=(
            jax.ShapeDtypeStruct((count, width), BF16),
            jax.ShapeDtypeStruct((rows_here, 8, local), F32),
        ),
        in_specs=[vmem] * 3,
        out_specs=(vmem, vmem),
        scratch_shapes=[
            halves, halves, halves,
            pltpu.VMEM((count, half), BF16), pltpu.VMEM((count, half), BF16),
            halves, halves, halves, halves,
            pltpu.VMEM((2, 2 * count, local), F32), pltpu.VMEM((2, 2 * count, local), F32),
            pltpu.VMEM((2, 3, count, local), BF16),
            pltpu.VMEM((2, heads, count, count), F32),
            pltpu.VMEM((2, count, local), BF16),
            pltpu.VMEM((2, 3, count, local), BF16),
            pltpu.VMEM((heads * count, count), BF16),
            pltpu.VMEM((2, heads * count, count), BF16),
            pltpu.VMEM((2, 4, 2, n // 2, rows_here, local), BF16),
            pltpu.VMEM((2, 4, n // 2, rows_here, local), BF16),
            pltpu.VMEM((2, 4, n // 2, rows_here, local), BF16),
            pltpu.VMEM((2, 4, n // 2, rows_here, local), BF16),
            dma((3, 2 * n)), dma((3, 2 * n)), dma((3,)), dma((3,)),
            dma((2, 4)), dma((2, 4)), dma((2, 4, n // 2)), dma((2, 4, n // 2)),
        ],
        compiler_params=pltpu.CompilerParams(
            collective_id=0, has_side_effects=True, vmem_limit_bytes=44 * 1024 * 1024
        ),
    )(latent[0], jnp.transpose(weights, (1, 0, 2)), cotangent[0])
    return (latent_grad[None], weight_grad)


def either(latent, weights, cotangent):
    n = lax.axis_size("row")
    rows, cols, width = latent.shape
    aligned = n % 2 == 0 and cols % (16 * n) == 0 and width % (16 * n) == 0
    if rows == 1 and aligned and lax.axis_size("head") == 2:
        return fused_call(latent, weights, cotangent)
    return on_device(latent, weights, cotangent)


def solution(mesh):
    in_specs = (P(("grp", "row"), None, None), P(None, None, "head"), P(("grp", "row"), None, None))
    out_specs = (P(("grp", "row"), None, None), P(("grp", "row"), None, "head"))
    return jax.shard_map(
        either, mesh=mesh, in_specs=in_specs, out_specs=out_specs, check_vma=False
    )
```

```python
import functools
import math

import jax
import jax.numpy as jnp
from jax import lax
from jax.experimental import pallas as pl
from jax.experimental.pallas import tpu as pltpu
from jax.sharding import PartitionSpec as P

HEAD_DIM = 64


epsilon = 1e-06


def index_pair(pattern):
    return (pattern + "hd", pattern.replace("l", "m") + "hd")


def head_norm(values):
    inverse = lax.rsqrt(jnp.mean(values * values, axis=-1, keepdims=True) + epsilon)
    return (values * inverse, inverse)


def three_maps(weights, first):
    width = weights.shape[0]
    return weights[:, first : first + 3, :].reshape(width, 3 * weights.shape[2])


def attend_local(inputs, weights, first, pattern):
    outer, inner, width = inputs.shape
    local = weights.shape[2]
    heads_here = local // HEAD_DIM
    logit_scale = 2.0 / math.sqrt(HEAD_DIM)
    flat = inputs.reshape(outer * inner, width)
    joined = jnp.dot(flat, three_maps(weights, first), preferred_element_type=jnp.float32)
    shaped = joined.reshape(outer, inner, 3, heads_here, HEAD_DIM)
    query_n, query_r = head_norm(shaped[:, :, 0])
    key_n, key_r = head_norm(shaped[:, :, 1])
    query_batched = query_n.astype(jnp.bfloat16)
    key_batched = key_n.astype(jnp.bfloat16)
    value_batched = shaped[:, :, 2].astype(jnp.bfloat16)
    query_ix, key_ix = index_pair(pattern)
    attention_logits = logit_scale * jnp.einsum(
        query_ix + "," + key_ix + "->shlm",
        query_batched,
        key_batched,
        preferred_element_type=jnp.float32,
    )
    expo = jnp.exp(attention_logits)
    probs = expo / jnp.sum(expo, axis=-1, keepdims=True)
    probability_batched = probs.astype(jnp.bfloat16)
    attention_output = jnp.einsum(
        "shlm," + key_ix + "->" + query_ix,
        probability_batched,
        value_batched,
        preferred_element_type=jnp.float32,
    ).astype(jnp.bfloat16)
    saved = (
        query_n,
        query_r,
        query_batched,
        key_n,
        key_r,
        key_batched,
        value_batched,
        probs,
        probability_batched,
    )
    return (flat, saved, attention_output.reshape(outer * inner, local))


def attend_back(saved, upstream, weights, first, pattern):
    outer, inner, width = upstream.shape
    local = weights.shape[2]
    heads_here = local // HEAD_DIM
    logit_scale = 2.0 / math.sqrt(HEAD_DIM)
    (
        query_n,
        query_r,
        query_batched,
        key_n,
        key_r,
        key_batched,
        value_batched,
        probs,
        probability_batched,
    ) = saved
    query_ix, key_ix = index_pair(pattern)
    grad_flat = upstream.reshape(outer * inner, width)
    grad_att = jnp.dot(
        grad_flat, weights[:, first + 3, :], preferred_element_type=jnp.float32
    ).astype(jnp.bfloat16)
    grad_att = grad_att.reshape(outer, inner, heads_here, HEAD_DIM)
    gradient_value_rows = jnp.einsum(
        "shlm," + query_ix + "->" + key_ix,
        probability_batched,
        grad_att,
        preferred_element_type=jnp.float32,
    ).astype(jnp.bfloat16)
    gradient_probability = jnp.einsum(
        query_ix + "," + key_ix + "->shlm",
        grad_att,
        value_batched,
        preferred_element_type=jnp.float32,
    )
    delta = jnp.sum(probs * gradient_probability, axis=-1, keepdims=True)
    gradient_logits = (probs * (gradient_probability - delta)).astype(jnp.bfloat16)
    gradient_normed_query = logit_scale * jnp.einsum(
        "shlm," + key_ix + "->" + query_ix,
        gradient_logits,
        key_batched,
        preferred_element_type=jnp.float32,
    )
    gradient_normed_key = logit_scale * jnp.einsum(
        "shlm," + query_ix + "->" + key_ix,
        gradient_logits,
        query_batched,
        preferred_element_type=jnp.float32,
    )
    grad_query = (
        query_r
        * (
            gradient_normed_query
            - query_n * jnp.mean(gradient_normed_query * query_n, axis=-1, keepdims=True)
        )
    ).astype(jnp.bfloat16)
    grad_key = (
        key_r
        * (
            gradient_normed_key
            - key_n * jnp.mean(gradient_normed_key * key_n, axis=-1, keepdims=True)
        )
    ).astype(jnp.bfloat16)
    stacked = jnp.stack([grad_query, grad_key, gradient_value_rows], axis=2).reshape(
        outer * inner, 3 * local
    )
    partial_in = lax.dot_general(
        stacked,
        three_maps(weights, first),
        (((1,), (1,)), ((), ())),
        preferred_element_type=jnp.float32,
    )
    return (partial_in, stacked, grad_flat)


def weight_terms(flat, stacked, grad_flat, attention_output, count):
    contract = (((0,), (0,)), ((), ()))
    three = lax.dot_general(flat, stacked, contract, preferred_element_type=jnp.float32)
    last = lax.dot_general(
        grad_flat, attention_output, contract, preferred_element_type=jnp.float32
    )
    return jnp.concatenate((three.reshape(count, 3, -1), last.reshape(count, 1, -1)), 1)


def head_sum(partial_value):
    return lax.psum(partial_value.astype(jnp.bfloat16), "head").astype(jnp.float32)


def on_device(latent, weights, cotangent):
    rows, cols, width = latent.shape
    rows_here = width // lax.axis_size("row")
    flat_row, saved_row, attended_row = attend_local(latent, weights, 0, "sl")
    mixed = head_sum(
        lax.dot_general(
            attended_row,
            weights[:, 3, :],
            (((1,), (1,)), ((), ())),
            preferred_element_type=jnp.float32,
        )
    )
    first_out = (latent.astype(jnp.float32) + mixed.reshape(rows, cols, width)).astype(jnp.bfloat16)
    columns, cotangent_cols = (
        lax.all_to_all(first_out, "row", split_axis=1, concat_axis=0, tiled=True),
        lax.all_to_all(cotangent, "row", split_axis=1, concat_axis=0, tiled=True),
    )
    height = columns.shape[0]
    flat_col, saved_col, attended_col = attend_local(columns, weights, 4, "ls")
    partial_col, stacked_col, grad_col = attend_back(saved_col, cotangent_cols, weights, 4, "ls")
    grad_mid = (
        cotangent_cols.astype(jnp.float32) + head_sum(partial_col).reshape(columns.shape)
    ).astype(jnp.bfloat16)
    grad_first = lax.all_to_all(grad_mid, "row", split_axis=0, concat_axis=1, tiled=True)
    partial_row, stacked_row, grad_row = attend_back(saved_row, grad_first, weights, 0, "sl")
    latent_grad = (
        grad_first.astype(jnp.float32) + head_sum(partial_row).reshape(latent.shape)
    ).astype(jnp.bfloat16)
    summed = lax.psum_scatter(
        jnp.concatenate(
            (
                weight_terms(
                    flat_row, stacked_row, grad_row, attended_row, rows_here * lax.axis_size("row")
                ),
                weight_terms(
                    flat_col, stacked_col, grad_col, attended_col, rows_here * lax.axis_size("row")
                ),
            ),
            1,
        ),
        "row",
        scatter_dimension=0,
        tiled=True,
    )
    weight_grad = summed * (1.0 / math.sqrt(height * cols))
    return (latent_grad, weight_grad)


MESH = pl.DeviceIdType.MESH
F32, BF16 = jnp.float32, jnp.bfloat16


def mm(left, right):
    return jnp.dot(left, right, preferred_element_type=F32)


def mm_t(left, right):
    return lax.dot_general(left, right, (((1,), (1,)), ((), ())), preferred_element_type=F32)


def t_mm(left, right):
    return lax.dot_general(left, right, (((0,), (0,)), ((), ())), preferred_element_type=F32)


def fused(
    n, scale, x_ref, w_ref, ct_ref, lat_ref, wg_ref,
    gcol, ycol, gmid, ysend, dsend, hsend, hrecv, fsend, frecv,
    norm_s, inv_s, qkv_s, probs_s, att_s, grads_s, dstack, pstack,
    xs, xr, zs, zr,
    a_send, a_recv, h_send, h_recv, x_send, x_recv, z_send, z_recv,
):
    me, core = lax.axis_index("row"), lax.axis_index("head")
    other = 1 - core
    count, width = x_ref.shape
    local = w_ref.shape[2]
    block, half = count // n, width // 2
    heads = local // HEAD_DIM
    logit_scale = 2.0 / math.sqrt(HEAD_DIM)
    pairs = n // 2
    my_x, my_z = lax.rem(me, 2), me // 2
    rows_here = width // n

    peers = [(me, other)]
    for step in range(1, n):
        for which in (core, other):
            peers.append((lax.rem(me + step, n), which))

    def rows_of(position):
        return pl.ds(pl.multiple_of(position * block, block), block)

    def half_of(which):
        return pl.ds(pl.multiple_of(which * half, half), half)

    def block_copy(phase, index, src, dst, source, target):
        row, which = source
        return pltpu.make_async_remote_copy(
            src_ref=src,
            dst_ref=dst.at[which, rows_of(row), :],
            send_sem=a_send.at[phase, index],
            recv_sem=a_recv.at[phase, which * n + row],
            device_id={"row": target[0], "head": target[1]},
            device_id_type=MESH,
        )

    def exchange_start(phase, view, dst):
        for step in range(1, n):
            row = lax.rem(me + step, n)
            block_copy(phase, step, view(row), dst, (me, core), (row, core)).start()
        block_copy(phase, n, view(me), dst, (me, core), (me, other)).start()

    def exchange_pass(phase, view, dst):
        for step in range(1, n):
            row = lax.rem(me + n - step, n)
            block_copy(phase, step, view(me), dst, (row, core), (row, core)).wait_recv()
            here = dst.at[core, rows_of(row), :]
            block_copy(phase, n + step, here, dst, (row, core), (me, other)).start()

    def exchange_wait(phase, view, dst):
        for step in range(n):
            row = lax.rem(me + n - step, n)
            block_copy(phase, step, view(me), dst, (row, other), (me, other)).wait_recv()

    def exchange_end(phase, view, dst):
        for index in range(1, 2 * n):
            block_copy(phase, index, view(me), dst, (me, core), (me, other)).wait_send()

    def head_copy(phase, src, dst):
        return pltpu.make_async_remote_copy(
            src_ref=src, dst_ref=dst, send_sem=h_send.at[phase], recv_sem=h_recv.at[phase],
            device_id={"row": me, "head": other}, device_id_type=MESH,
        )

    def x_copy(layer, slot):
        return pltpu.make_async_remote_copy(
            src_ref=xs.at[layer, slot, 1 - my_x], dst_ref=xr.at[layer, slot],
            send_sem=x_send.at[layer, slot], recv_sem=x_recv.at[layer, slot],
            device_id={"row": me + 1 - 2 * my_x, "head": core}, device_id_type=MESH,
        )

    def z_copy(layer, slot, index, source_z, target_z):
        return pltpu.make_async_remote_copy(
            src_ref=zs.at[layer, slot, target_z], dst_ref=zr.at[layer, slot, source_z],
            send_sem=z_send.at[layer, slot, index], recv_sem=z_recv.at[layer, slot, source_z],
            device_id={"row": 2 * target_z + my_x, "head": core}, device_id_type=MESH,
        )

    def scatter_first(layer, slot, product):
        rounded = product.astype(BF16)
        for target in range(n):
            xs[layer, slot, target % 2, target // 2] = rounded[
                target * rows_here : (target + 1) * rows_here
            ]
        x_copy(layer, slot).start()

    def scatter_second(layer, slot):
        x_copy(layer, slot).wait_recv()
        total = xs[layer, slot, my_x].astype(F32) + xr[layer, slot].astype(F32)
        zs[layer, slot] = total.astype(BF16)
        for step in range(1, pairs):
            z_copy(layer, slot, step, my_z, lax.rem(my_z + step, pairs)).start()

    def scatter_last(layer, slot):
        total = zs[layer, slot, my_z].astype(F32)
        for step in range(1, pairs):
            source = lax.rem(my_z + step, pairs)
            z_copy(layer, slot, step, source, source).wait_recv()
            total = total + zr[layer, slot, source].astype(F32)
        wg_ref[:, 4 * layer + slot, :] = total * scale

    lane = lax.broadcasted_iota(jnp.int32, (1, local), 1) // HEAD_DIM
    head_mask = [jnp.where(lane == head, 1.0, 0.0).astype(BF16) for head in range(heads)]
    spread = jnp.where(
        lax.broadcasted_iota(jnp.int32, (local, local), 0) // HEAD_DIM
        == lax.broadcasted_iota(jnp.int32, (local, local), 1) // HEAD_DIM,
        1.0 / HEAD_DIM, 0.0,
    ).astype(BF16)
    spread_twice = jnp.concatenate([spread, spread], 0)

    def head_mean(values):
        high = values.astype(BF16)
        low = (values - high.astype(F32)).astype(BF16)
        return mm(jnp.concatenate([high, low], 1), spread_twice)

    def masked(values):
        return jnp.concatenate([values * mask for mask in head_mask], 0)

    def forward(layer, z):
        query, key, value = (mm(z, w_ref[4 * layer + i]) for i in range(3))
        both = jnp.concatenate([query, key], 0)
        inverse = lax.rsqrt(head_mean(both * both) + epsilon)
        normed = both * inverse
        norm_s[layer] = normed
        inv_s[layer] = inverse
        qkv_s[layer, 0] = normed[:count].astype(BF16)
        qkv_s[layer, 1] = normed[count:].astype(BF16)
        qkv_s[layer, 2] = value.astype(BF16)
        query_b, key_b = qkv_s[layer, 0], qkv_s[layer, 1]
        keep = None
        if layer == 1:
            keep = jnp.where(
                lax.rem(lax.broadcasted_iota(jnp.int32, (count, count), 0), block)
                == lax.rem(lax.broadcasted_iota(jnp.int32, (count, count), 1), block),
                1.0, 0.0,
            )
        for head in range(heads):
            expo = jnp.exp(logit_scale * mm_t(query_b * head_mask[head], key_b))
            if keep is not None:
                expo = expo * keep
            probs = expo * (1.0 / jnp.sum(expo, axis=-1, keepdims=True))
            probs_s[layer, head] = probs
            pstack[layer, head * count : (head + 1) * count, :] = probs.astype(BF16)
        wide = jnp.concatenate(
            [pstack[layer, head * count : (head + 1) * count, :] for head in range(heads)], 1
        )
        att_s[layer] = mm(wide, masked(qkv_s[layer, 2])).astype(BF16)

    def backward(layer, grad, after_value):
        query_b, key_b, value_b = qkv_s[layer, 0], qkv_s[layer, 1], qkv_s[layer, 2]
        grad_att = mm(grad, w_ref[4 * layer + 3]).astype(BF16)
        grads_s[layer, 2] = t_mm(pstack[layer], masked(grad_att)).astype(BF16)
        after_value()
        for head in range(heads):
            grad_probs = mm_t(grad_att * head_mask[head], value_b)
            probs = probs_s[layer, head]
            delta = jnp.sum(probs * grad_probs, axis=-1, keepdims=True)
            dstack[head * count : (head + 1) * count, :] = (
                probs * (grad_probs - delta)
            ).astype(BF16)
        wide = jnp.concatenate(
            [dstack[head * count : (head + 1) * count, :] for head in range(heads)], 1
        )
        grad_query = mm(wide, masked(key_b))
        grad_key = t_mm(dstack[...], masked(query_b))
        grads = logit_scale * jnp.concatenate([grad_query, grad_key], 0)
        normed = norm_s[layer]
        out = (inv_s[layer] * (grads - normed * head_mean(grads * normed))).astype(BF16)
        grads_s[layer, 0] = out[:count]
        grads_s[layer, 1] = out[count:]

    def input_grad(layer, which):
        total = mm_t(grads_s[layer, 0], w_ref[4 * layer, half_of(which), :])
        for i in (1, 2):
            total = total + mm_t(grads_s[layer, i], w_ref[4 * layer + i, half_of(which), :])
        return total

    def joined(ref):
        return jnp.concatenate([ref[0], ref[1]], 1)

    barrier = pltpu.get_barrier_semaphore()
    for row, which in peers:
        pl.semaphore_signal(
            barrier, inc=1, device_id={"row": row, "head": which}, device_id_type=MESH
        )
    pl.semaphore_wait(barrier, len(peers))

    def ct_view(row):
        return ct_ref.at[rows_of(row), half_of(core)]

    def y_view(row):
        return ysend.at[rows_of(row), :]

    def d_view(row):
        return dsend.at[rows_of(row), :]

    exchange_start(0, ct_view, gcol)
    gcol[core, rows_of(me), :] = ct_ref[rows_of(me), half_of(core)]

    forward(0, x_ref[...])
    hsend[0] = mm_t(att_s[0], w_ref[3, half_of(other), :]).astype(BF16)
    first_half = head_copy(0, hsend.at[0], hrecv.at[0])
    first_half.start()
    mixed = mm_t(att_s[0], w_ref[3, half_of(core), :]) + x_ref[:, half_of(core)].astype(F32)
    first_half.wait_recv()
    ysend[...] = (mixed + hrecv[0].astype(F32)).astype(BF16)
    exchange_start(1, y_view, ycol)
    ycol[core, rows_of(me), :] = ysend[rows_of(me), :]

    exchange_pass(0, ct_view, gcol)
    exchange_pass(1, y_view, ycol)
    exchange_wait(0, ct_view, gcol)
    exchange_wait(1, y_view, ycol)
    columns = joined(ycol)
    forward(1, columns)
    scatter_first(1, 3, mm(joined(gcol).T, att_s[1]))
    turned = columns.T
    backward(1, joined(gcol), lambda: scatter_first(1, 2, mm(turned, grads_s[1, 2])))
    hsend[1] = input_grad(1, other).astype(BF16)
    second_half = head_copy(1, hsend.at[1], hrecv.at[1])
    second_half.start()
    mixed = input_grad(1, core) + gcol[core].astype(F32)
    second_half.wait_recv()
    dsend[...] = (mixed + hrecv[1].astype(F32)).astype(BF16)
    exchange_start(2, d_view, gmid)
    gmid[core, rows_of(me), :] = dsend[rows_of(me), :]
    for slot in range(2):
        scatter_first(1, slot, mm(turned, grads_s[1, slot]))
    for slot in (3, 2):
        scatter_second(1, slot)

    exchange_pass(2, d_view, gmid)
    exchange_wait(2, d_view, gmid)
    grad_first = joined(gmid)
    scatter_first(0, 3, mm(grad_first.T, att_s[0]))

    turned = x_ref[...].T
    backward(0, grad_first, lambda: scatter_first(0, 2, mm(turned, grads_s[0, 2])))
    scatter_first(0, 0, mm(turned, grads_s[0, 0]))
    scatter_first(0, 1, mm(turned, grads_s[0, 1]))
    for which in range(2):
        fsend[which] = input_grad(0, which).astype(BF16)
    full = head_copy(2, fsend, frecv)
    full.start()
    scatter_second(1, 0)
    scatter_second(1, 1)
    scatter_second(0, 3)
    scatter_second(0, 2)
    full.wait_recv()
    for which in range(2):
        lat_ref[:, which * half : (which + 1) * half] = (
            gmid[which].astype(F32) + (fsend[which].astype(F32) + frecv[which].astype(F32))
        ).astype(BF16)
    for slot in range(4):
        scatter_last(1, slot)
    scatter_second(0, 0)
    scatter_second(0, 1)
    for slot in (3, 2, 0, 1):
        scatter_last(0, slot)

    exchange_end(0, ct_view, gcol)
    exchange_end(1, y_view, ycol)
    exchange_end(2, d_view, gmid)
    for copy in (first_half, second_half, full):
        copy.wait_send()
    for layer in range(2):
        for slot in range(4):
            x_copy(layer, slot).wait_send()
            for step in range(1, pairs):
                z_copy(layer, slot, step, my_z, lax.rem(my_z + step, pairs)).wait_send()


def fused_call(latent, weights, cotangent):
    n = lax.axis_size("row")
    _, count, width = latent.shape
    local = weights.shape[2]
    heads, block, half, rows_here = local // HEAD_DIM, count // n, width // 2, width // n
    scale = 1.0 / math.sqrt(n * count)
    vmem = pl.BlockSpec(memory_space=pltpu.VMEM)
    dma = pltpu.SemaphoreType.DMA
    halves = pltpu.VMEM((2, count, half), BF16)
    latent_grad, weight_grad = pl.pallas_call(
        functools.partial(fused, n, scale),
        out_shape=(
            jax.ShapeDtypeStruct((count, width), BF16),
            jax.ShapeDtypeStruct((rows_here, 8, local), F32),
        ),
        in_specs=[vmem] * 3,
        out_specs=(vmem, vmem),
        scratch_shapes=[
            halves, halves, halves,
            pltpu.VMEM((count, half), BF16), pltpu.VMEM((count, half), BF16),
            halves, halves, halves, halves,
            pltpu.VMEM((2, 2 * count, local), F32), pltpu.VMEM((2, 2 * count, local), F32),
            pltpu.VMEM((2, 3, count, local), BF16),
            pltpu.VMEM((2, heads, count, count), F32),
            pltpu.VMEM((2, count, local), BF16),
            pltpu.VMEM((2, 3, count, local), BF16),
            pltpu.VMEM((heads * count, count), BF16),
            pltpu.VMEM((2, heads * count, count), BF16),
            pltpu.VMEM((2, 4, 2, n // 2, rows_here, local), BF16),
            pltpu.VMEM((2, 4, n // 2, rows_here, local), BF16),
            pltpu.VMEM((2, 4, n // 2, rows_here, local), BF16),
            pltpu.VMEM((2, 4, n // 2, rows_here, local), BF16),
            dma((3, 2 * n)), dma((3, 2 * n)), dma((3,)), dma((3,)),
            dma((2, 4)), dma((2, 4)), dma((2, 4, n // 2)), dma((2, 4, n // 2)),
        ],
        compiler_params=pltpu.CompilerParams(
            collective_id=0, has_side_effects=True, vmem_limit_bytes=44 * 1024 * 1024
        ),
    )(latent[0], jnp.transpose(weights, (1, 0, 2)), cotangent[0])
    return (latent_grad[None], weight_grad)


def either(latent, weights, cotangent):
    n = lax.axis_size("row")
    rows, cols, width = latent.shape
    aligned = n % 2 == 0 and cols % (16 * n) == 0 and width % (16 * n) == 0
    if rows == 1 and aligned and lax.axis_size("head") == 2:
        return fused_call(latent, weights, cotangent)
    return on_device(latent, weights, cotangent)


def solution(mesh):
    in_specs = (P(("grp", "row"), None, None), P(None, None, "head"), P(("grp", "row"), None, None))
    out_specs = (P(("grp", "row"), None, None), P(("grp", "row"), None, "head"))
    return jax.shard_map(
        either, mesh=mesh, in_specs=in_specs, out_specs=out_specs, check_vma=False
    )
```

```python
import functools
import math

import jax
import jax.numpy as jnp
from jax import lax
from jax.experimental import pallas as pl
from jax.experimental.pallas import tpu as pltpu
from jax.sharding import PartitionSpec as P

HEAD_DIM = 64


epsilon = 1e-06


def index_pair(pattern):
    return (pattern + "hd", pattern.replace("l", "m") + "hd")


def head_norm(values):
    inverse = lax.rsqrt(jnp.mean(values * values, axis=-1, keepdims=True) + epsilon)
    return (values * inverse, inverse)


def three_maps(weights, first):
    width = weights.shape[0]
    return weights[:, first : first + 3, :].reshape(width, 3 * weights.shape[2])


def attend_local(inputs, weights, first, pattern):
    outer, inner, width = inputs.shape
    local = weights.shape[2]
    heads_here = local // HEAD_DIM
    logit_scale = 2.0 / math.sqrt(HEAD_DIM)
    flat = inputs.reshape(outer * inner, width)
    joined = jnp.dot(flat, three_maps(weights, first), preferred_element_type=jnp.float32)
    shaped = joined.reshape(outer, inner, 3, heads_here, HEAD_DIM)
    query_n, query_r = head_norm(shaped[:, :, 0])
    key_n, key_r = head_norm(shaped[:, :, 1])
    query_batched = query_n.astype(jnp.bfloat16)
    key_batched = key_n.astype(jnp.bfloat16)
    value_batched = shaped[:, :, 2].astype(jnp.bfloat16)
    query_ix, key_ix = index_pair(pattern)
    attention_logits = logit_scale * jnp.einsum(
        query_ix + "," + key_ix + "->shlm",
        query_batched,
        key_batched,
        preferred_element_type=jnp.float32,
    )
    expo = jnp.exp(attention_logits)
    probs = expo / jnp.sum(expo, axis=-1, keepdims=True)
    probability_batched = probs.astype(jnp.bfloat16)
    attention_output = jnp.einsum(
        "shlm," + key_ix + "->" + query_ix,
        probability_batched,
        value_batched,
        preferred_element_type=jnp.float32,
    ).astype(jnp.bfloat16)
    saved = (
        query_n,
        query_r,
        query_batched,
        key_n,
        key_r,
        key_batched,
        value_batched,
        probs,
        probability_batched,
    )
    return (flat, saved, attention_output.reshape(outer * inner, local))


def attend_back(saved, upstream, weights, first, pattern):
    outer, inner, width = upstream.shape
    local = weights.shape[2]
    heads_here = local // HEAD_DIM
    logit_scale = 2.0 / math.sqrt(HEAD_DIM)
    (
        query_n,
        query_r,
        query_batched,
        key_n,
        key_r,
        key_batched,
        value_batched,
        probs,
        probability_batched,
    ) = saved
    query_ix, key_ix = index_pair(pattern)
    grad_flat = upstream.reshape(outer * inner, width)
    grad_att = jnp.dot(
        grad_flat, weights[:, first + 3, :], preferred_element_type=jnp.float32
    ).astype(jnp.bfloat16)
    grad_att = grad_att.reshape(outer, inner, heads_here, HEAD_DIM)
    gradient_value_rows = jnp.einsum(
        "shlm," + query_ix + "->" + key_ix,
        probability_batched,
        grad_att,
        preferred_element_type=jnp.float32,
    ).astype(jnp.bfloat16)
    gradient_probability = jnp.einsum(
        query_ix + "," + key_ix + "->shlm",
        grad_att,
        value_batched,
        preferred_element_type=jnp.float32,
    )
    delta = jnp.sum(probs * gradient_probability, axis=-1, keepdims=True)
    gradient_logits = (probs * (gradient_probability - delta)).astype(jnp.bfloat16)
    gradient_normed_query = logit_scale * jnp.einsum(
        "shlm," + key_ix + "->" + query_ix,
        gradient_logits,
        key_batched,
        preferred_element_type=jnp.float32,
    )
    gradient_normed_key = logit_scale * jnp.einsum(
        "shlm," + query_ix + "->" + key_ix,
        gradient_logits,
        query_batched,
        preferred_element_type=jnp.float32,
    )
    grad_query = (
        query_r
        * (
            gradient_normed_query
            - query_n * jnp.mean(gradient_normed_query * query_n, axis=-1, keepdims=True)
        )
    ).astype(jnp.bfloat16)
    grad_key = (
        key_r
        * (
            gradient_normed_key
            - key_n * jnp.mean(gradient_normed_key * key_n, axis=-1, keepdims=True)
        )
    ).astype(jnp.bfloat16)
    stacked = jnp.stack([grad_query, grad_key, gradient_value_rows], axis=2).reshape(
        outer * inner, 3 * local
    )
    partial_in = lax.dot_general(
        stacked,
        three_maps(weights, first),
        (((1,), (1,)), ((), ())),
        preferred_element_type=jnp.float32,
    )
    return (partial_in, stacked, grad_flat)


def weight_terms(flat, stacked, grad_flat, attention_output, count):
    contract = (((0,), (0,)), ((), ()))
    three = lax.dot_general(flat, stacked, contract, preferred_element_type=jnp.float32)
    last = lax.dot_general(
        grad_flat, attention_output, contract, preferred_element_type=jnp.float32
    )
    return jnp.concatenate((three.reshape(count, 3, -1), last.reshape(count, 1, -1)), 1)


def head_sum(partial_value):
    return lax.psum(partial_value.astype(jnp.bfloat16), "head").astype(jnp.float32)


def on_device(latent, weights, cotangent):
    rows, cols, width = latent.shape
    rows_here = width // lax.axis_size("row")
    flat_row, saved_row, attended_row = attend_local(latent, weights, 0, "sl")
    mixed = head_sum(
        lax.dot_general(
            attended_row,
            weights[:, 3, :],
            (((1,), (1,)), ((), ())),
            preferred_element_type=jnp.float32,
        )
    )
    first_out = (latent.astype(jnp.float32) + mixed.reshape(rows, cols, width)).astype(jnp.bfloat16)
    columns, cotangent_cols = (
        lax.all_to_all(first_out, "row", split_axis=1, concat_axis=0, tiled=True),
        lax.all_to_all(cotangent, "row", split_axis=1, concat_axis=0, tiled=True),
    )
    height = columns.shape[0]
    flat_col, saved_col, attended_col = attend_local(columns, weights, 4, "ls")
    partial_col, stacked_col, grad_col = attend_back(saved_col, cotangent_cols, weights, 4, "ls")
    grad_mid = (
        cotangent_cols.astype(jnp.float32) + head_sum(partial_col).reshape(columns.shape)
    ).astype(jnp.bfloat16)
    grad_first = lax.all_to_all(grad_mid, "row", split_axis=0, concat_axis=1, tiled=True)
    partial_row, stacked_row, grad_row = attend_back(saved_row, grad_first, weights, 0, "sl")
    latent_grad = (
        grad_first.astype(jnp.float32) + head_sum(partial_row).reshape(latent.shape)
    ).astype(jnp.bfloat16)
    summed = lax.psum_scatter(
        jnp.concatenate(
            (
                weight_terms(
                    flat_row, stacked_row, grad_row, attended_row, rows_here * lax.axis_size("row")
                ),
                weight_terms(
                    flat_col, stacked_col, grad_col, attended_col, rows_here * lax.axis_size("row")
                ),
            ),
            1,
        ),
        "row",
        scatter_dimension=0,
        tiled=True,
    )
    weight_grad = summed * (1.0 / math.sqrt(height * cols))
    return (latent_grad, weight_grad)


MESH = pl.DeviceIdType.MESH
F32, BF16 = jnp.float32, jnp.bfloat16


def mm(left, right):
    return jnp.dot(left, right, preferred_element_type=F32)


def mm_t(left, right):
    return lax.dot_general(left, right, (((1,), (1,)), ((), ())), preferred_element_type=F32)


def t_mm(left, right):
    return lax.dot_general(left, right, (((0,), (0,)), ((), ())), preferred_element_type=F32)


def fused(
    n, scale, x_ref, w_ref, ct_ref, lat_ref, wg_ref,
    gcol, ycol, gmid, ysend, dsend, hsend, hrecv, fsend, frecv,
    norm_s, inv_s, qkv_s, probs_s, att_s, grads_s, dstack, pstack,
    xs, xr, zs, zr,
    a_send, a_recv, h_send, h_recv, x_send, x_recv, z_send, z_recv,
):
    me, core = lax.axis_index("row"), lax.axis_index("head")
    other = 1 - core
    count, width = x_ref.shape
    local = w_ref.shape[2]
    block, half = count // n, width // 2
    heads = local // HEAD_DIM
    logit_scale = 2.0 / math.sqrt(HEAD_DIM)
    pairs = n // 2
    my_x, my_z = lax.rem(me, 2), me // 2
    rows_here = width // n

    peers = [(me, other)]
    for step in range(1, n):
        for which in (core, other):
            peers.append((lax.rem(me + step, n), which))

    def rows_of(position):
        return pl.ds(pl.multiple_of(position * block, block), block)

    def half_of(which):
        return pl.ds(pl.multiple_of(which * half, half), half)

    def block_copy(phase, index, src, dst, source, target):
        row, which = source
        return pltpu.make_async_remote_copy(
            src_ref=src,
            dst_ref=dst.at[which, rows_of(row), :],
            send_sem=a_send.at[phase, index],
            recv_sem=a_recv.at[phase, which * n + row],
            device_id={"row": target[0], "head": target[1]},
            device_id_type=MESH,
        )

    def exchange_start(phase, view, dst):
        for step in range(1, n):
            row = lax.rem(me + step, n)
            block_copy(phase, step, view(row), dst, (me, core), (row, core)).start()
        block_copy(phase, n, view(me), dst, (me, core), (me, other)).start()

    def exchange_pass(phase, view, dst):
        for step in range(1, n):
            row = lax.rem(me + n - step, n)
            block_copy(phase, step, view(me), dst, (row, core), (row, core)).wait_recv()
            here = dst.at[core, rows_of(row), :]
            block_copy(phase, n + step, here, dst, (row, core), (me, other)).start()

    def exchange_wait(phase, view, dst):
        for step in range(n):
            row = lax.rem(me + n - step, n)
            block_copy(phase, step, view(me), dst, (row, other), (me, other)).wait_recv()

    def exchange_end(phase, view, dst):
        for index in range(1, 2 * n):
            block_copy(phase, index, view(me), dst, (me, core), (me, other)).wait_send()

    def head_copy(phase, src, dst):
        return pltpu.make_async_remote_copy(
            src_ref=src, dst_ref=dst, send_sem=h_send.at[phase], recv_sem=h_recv.at[phase],
            device_id={"row": me, "head": other}, device_id_type=MESH,
        )

    def x_copy(layer, slot):
        return pltpu.make_async_remote_copy(
            src_ref=xs.at[layer, slot, 1 - my_x], dst_ref=xr.at[layer, slot],
            send_sem=x_send.at[layer, slot], recv_sem=x_recv.at[layer, slot],
            device_id={"row": me + 1 - 2 * my_x, "head": core}, device_id_type=MESH,
        )

    def z_copy(layer, slot, index, source_z, target_z):
        return pltpu.make_async_remote_copy(
            src_ref=zs.at[layer, slot, target_z], dst_ref=zr.at[layer, slot, source_z],
            send_sem=z_send.at[layer, slot, index], recv_sem=z_recv.at[layer, slot, source_z],
            device_id={"row": 2 * target_z + my_x, "head": core}, device_id_type=MESH,
        )

    def scatter_first(layer, slot, product):
        rounded = product.astype(BF16)
        for target in range(n):
            xs[layer, slot, target % 2, target // 2] = rounded[
                target * rows_here : (target + 1) * rows_here
            ]
        x_copy(layer, slot).start()

    def scatter_second(layer, slot):
        x_copy(layer, slot).wait_recv()
        total = xs[layer, slot, my_x].astype(F32) + xr[layer, slot].astype(F32)
        zs[layer, slot] = total.astype(BF16)
        for step in range(1, pairs):
            z_copy(layer, slot, step, my_z, lax.rem(my_z + step, pairs)).start()

    def scatter_last(layer, slot):
        total = zs[layer, slot, my_z].astype(F32)
        for step in range(1, pairs):
            source = lax.rem(my_z + step, pairs)
            z_copy(layer, slot, step, source, source).wait_recv()
            total = total + zr[layer, slot, source].astype(F32)
        wg_ref[:, 4 * layer + slot, :] = total * scale

    lane = lax.broadcasted_iota(jnp.int32, (1, local), 1) // HEAD_DIM
    head_mask = [jnp.where(lane == head, 1.0, 0.0).astype(BF16) for head in range(heads)]
    spread = jnp.where(
        lax.broadcasted_iota(jnp.int32, (local, local), 0) // HEAD_DIM
        == lax.broadcasted_iota(jnp.int32, (local, local), 1) // HEAD_DIM,
        1.0 / HEAD_DIM, 0.0,
    ).astype(BF16)
    spread_twice = jnp.concatenate([spread, spread], 0)

    def head_mean(values):
        high = values.astype(BF16)
        low = (values - high.astype(F32)).astype(BF16)
        return mm(jnp.concatenate([high, low], 1), spread_twice)

    def masked(values):
        return jnp.concatenate([values * mask for mask in head_mask], 0)

    def forward(layer, z):
        query, key, value = (mm(z, w_ref[4 * layer + i]) for i in range(3))
        both = jnp.concatenate([query, key], 0)
        inverse = lax.rsqrt(head_mean(both * both) + epsilon)
        normed = both * inverse
        norm_s[layer] = normed
        inv_s[layer] = inverse
        qkv_s[layer, 0] = normed[:count].astype(BF16)
        qkv_s[layer, 1] = normed[count:].astype(BF16)
        qkv_s[layer, 2] = value.astype(BF16)
        query_b, key_b = qkv_s[layer, 0], qkv_s[layer, 1]
        keep = None
        if layer == 1:
            keep = jnp.where(
                lax.rem(lax.broadcasted_iota(jnp.int32, (count, count), 0), block)
                == lax.rem(lax.broadcasted_iota(jnp.int32, (count, count), 1), block),
                1.0, 0.0,
            )
        for head in range(heads):
            expo = jnp.exp(logit_scale * mm_t(query_b * head_mask[head], key_b))
            if keep is not None:
                expo = expo * keep
            probs = expo * (1.0 / jnp.sum(expo, axis=-1, keepdims=True))
            probs_s[layer, head] = probs
            pstack[layer, head * count : (head + 1) * count, :] = probs.astype(BF16)
        wide = jnp.concatenate(
            [pstack[layer, head * count : (head + 1) * count, :] for head in range(heads)], 1
        )
        att_s[layer] = mm(wide, masked(qkv_s[layer, 2])).astype(BF16)

    def backward(layer, grad, after_value):
        query_b, key_b, value_b = qkv_s[layer, 0], qkv_s[layer, 1], qkv_s[layer, 2]
        grad_att = mm(grad, w_ref[4 * layer + 3]).astype(BF16)
        grads_s[layer, 2] = t_mm(pstack[layer], masked(grad_att)).astype(BF16)
        after_value()
        for head in range(heads):
            grad_probs = mm_t(grad_att * head_mask[head], value_b)
            probs = probs_s[layer, head]
            delta = jnp.sum(probs * grad_probs, axis=-1, keepdims=True)
            dstack[head * count : (head + 1) * count, :] = (
                probs * (grad_probs - delta)
            ).astype(BF16)
        wide = jnp.concatenate(
            [dstack[head * count : (head + 1) * count, :] for head in range(heads)], 1
        )
        grad_query = mm(wide, masked(key_b))
        grad_key = t_mm(dstack[...], masked(query_b))
        grads = logit_scale * jnp.concatenate([grad_query, grad_key], 0)
        normed = norm_s[layer]
        out = (inv_s[layer] * (grads - normed * head_mean(grads * normed))).astype(BF16)
        grads_s[layer, 0] = out[:count]
        grads_s[layer, 1] = out[count:]

    def input_grad(layer, which):
        total = mm_t(grads_s[layer, 0], w_ref[4 * layer, half_of(which), :])
        for i in (1, 2):
            total = total + mm_t(grads_s[layer, i], w_ref[4 * layer + i, half_of(which), :])
        return total

    def joined(ref):
        return jnp.concatenate([ref[0], ref[1]], 1)

    barrier = pltpu.get_barrier_semaphore()
    for row, which in peers:
        pl.semaphore_signal(
            barrier, inc=1, device_id={"row": row, "head": which}, device_id_type=MESH
        )
    pl.semaphore_wait(barrier, len(peers))

    def ct_view(row):
        return ct_ref.at[rows_of(row), half_of(core)]

    def y_view(row):
        return ysend.at[rows_of(row), :]

    def d_view(row):
        return dsend.at[rows_of(row), :]

    exchange_start(0, ct_view, gcol)
    gcol[core, rows_of(me), :] = ct_ref[rows_of(me), half_of(core)]

    forward(0, x_ref[...])
    hsend[0] = mm_t(att_s[0], w_ref[3, half_of(other), :]).astype(BF16)
    first_half = head_copy(0, hsend.at[0], hrecv.at[0])
    first_half.start()
    mixed = mm_t(att_s[0], w_ref[3, half_of(core), :]) + x_ref[:, half_of(core)].astype(F32)
    first_half.wait_recv()
    ysend[...] = (mixed + hrecv[0].astype(F32)).astype(BF16)
    exchange_start(1, y_view, ycol)
    ycol[core, rows_of(me), :] = ysend[rows_of(me), :]

    exchange_pass(0, ct_view, gcol)
    exchange_pass(1, y_view, ycol)
    exchange_wait(0, ct_view, gcol)
    exchange_wait(1, y_view, ycol)
    columns = joined(ycol)
    forward(1, columns)
    scatter_first(1, 3, mm(joined(gcol).T, att_s[1]))
    turned = columns.T
    backward(1, joined(gcol), lambda: scatter_first(1, 2, mm(turned, grads_s[1, 2])))
    hsend[1] = input_grad(1, other).astype(BF16)
    second_half = head_copy(1, hsend.at[1], hrecv.at[1])
    second_half.start()
    mixed = input_grad(1, core) + gcol[core].astype(F32)
    second_half.wait_recv()
    dsend[...] = (mixed + hrecv[1].astype(F32)).astype(BF16)
    exchange_start(2, d_view, gmid)
    gmid[core, rows_of(me), :] = dsend[rows_of(me), :]
    for slot in range(2):
        scatter_first(1, slot, mm(turned, grads_s[1, slot]))
    for slot in (3, 2):
        scatter_second(1, slot)

    exchange_pass(2, d_view, gmid)
    exchange_wait(2, d_view, gmid)
    grad_first = joined(gmid)
    scatter_first(0, 3, mm(grad_first.T, att_s[0]))

    turned = x_ref[...].T
    backward(0, grad_first, lambda: scatter_first(0, 2, mm(turned, grads_s[0, 2])))
    scatter_second(1, 0)
    scatter_second(1, 1)
    scatter_first(0, 0, mm(turned, grads_s[0, 0]))
    scatter_first(0, 1, mm(turned, grads_s[0, 1]))
    scatter_second(0, 3)
    for which in range(2):
        fsend[which] = input_grad(0, which).astype(BF16)
    full = head_copy(2, fsend, frecv)
    full.start()
    scatter_second(0, 2)
    full.wait_recv()
    for which in range(2):
        lat_ref[:, which * half : (which + 1) * half] = (
            gmid[which].astype(F32) + (fsend[which].astype(F32) + frecv[which].astype(F32))
        ).astype(BF16)
    for slot in range(4):
        scatter_last(1, slot)
    scatter_second(0, 0)
    scatter_second(0, 1)
    for slot in (3, 2, 0, 1):
        scatter_last(0, slot)

    exchange_end(0, ct_view, gcol)
    exchange_end(1, y_view, ycol)
    exchange_end(2, d_view, gmid)
    for copy in (first_half, second_half, full):
        copy.wait_send()
    for layer in range(2):
        for slot in range(4):
            x_copy(layer, slot).wait_send()
            for step in range(1, pairs):
                z_copy(layer, slot, step, my_z, lax.rem(my_z + step, pairs)).wait_send()


def fused_call(latent, weights, cotangent):
    n = lax.axis_size("row")
    _, count, width = latent.shape
    local = weights.shape[2]
    heads, block, half, rows_here = local // HEAD_DIM, count // n, width // 2, width // n
    scale = 1.0 / math.sqrt(n * count)
    vmem = pl.BlockSpec(memory_space=pltpu.VMEM)
    dma = pltpu.SemaphoreType.DMA
    halves = pltpu.VMEM((2, count, half), BF16)
    latent_grad, weight_grad = pl.pallas_call(
        functools.partial(fused, n, scale),
        out_shape=(
            jax.ShapeDtypeStruct((count, width), BF16),
            jax.ShapeDtypeStruct((rows_here, 8, local), F32),
        ),
        in_specs=[vmem] * 3,
        out_specs=(vmem, vmem),
        scratch_shapes=[
            halves, halves, halves,
            pltpu.VMEM((count, half), BF16), pltpu.VMEM((count, half), BF16),
            halves, halves, halves, halves,
            pltpu.VMEM((2, 2 * count, local), F32), pltpu.VMEM((2, 2 * count, local), F32),
            pltpu.VMEM((2, 3, count, local), BF16),
            pltpu.VMEM((2, heads, count, count), F32),
            pltpu.VMEM((2, count, local), BF16),
            pltpu.VMEM((2, 3, count, local), BF16),
            pltpu.VMEM((heads * count, count), BF16),
            pltpu.VMEM((2, heads * count, count), BF16),
            pltpu.VMEM((2, 4, 2, n // 2, rows_here, local), BF16),
            pltpu.VMEM((2, 4, n // 2, rows_here, local), BF16),
            pltpu.VMEM((2, 4, n // 2, rows_here, local), BF16),
            pltpu.VMEM((2, 4, n // 2, rows_here, local), BF16),
            dma((3, 2 * n)), dma((3, 2 * n)), dma((3,)), dma((3,)),
            dma((2, 4)), dma((2, 4)), dma((2, 4, n // 2)), dma((2, 4, n // 2)),
        ],
        compiler_params=pltpu.CompilerParams(
            collective_id=0, has_side_effects=True, vmem_limit_bytes=44 * 1024 * 1024
        ),
    )(latent[0], jnp.transpose(weights, (1, 0, 2)), cotangent[0])
    return (latent_grad[None], weight_grad)


def either(latent, weights, cotangent):
    n = lax.axis_size("row")
    rows, cols, width = latent.shape
    aligned = n % 2 == 0 and cols % (16 * n) == 0 and width % (16 * n) == 0
    if rows == 1 and aligned and lax.axis_size("head") == 2:
        return fused_call(latent, weights, cotangent)
    return on_device(latent, weights, cotangent)


def solution(mesh):
    in_specs = (P(("grp", "row"), None, None), P(None, None, "head"), P(("grp", "row"), None, None))
    out_specs = (P(("grp", "row"), None, None), P(("grp", "row"), None, "head"))
    return jax.shard_map(
        either, mesh=mesh, in_specs=in_specs, out_specs=out_specs, check_vma=False
    )
```
